128 devices in a mesh: row: 32 (over z, y, core), col: 4 (over x).
Axes of the slice: x: 4, y: 4, z: 4, core: 2. Of those that a mesh axis runs over, the one named last changes fastest.
Arguments:
- cross_cov: bfloat16 [49152, 6144], P('row', 'col'), may hold values from -0.15917969 to 0.15917969
- diag_inverse: bfloat16 [2, 1536, 1536], replicated, as said below
- factor_u: bfloat16 [2, 49152, 384], P(None, 'row'), may hold values from -0.3125 to 0.3125
- factor_v: bfloat16 [2, 49152, 384], P(None, 'row'), may hold values from -0.15625 to 0.15625
- rank_ids: int32 [32, 2], P('row'), may hold values from 0 to 11
- weights_obs: float32 [3072], replicated, may hold values from -6 to 6
- observations: float32 [49152], P('row'), may hold values from -6 to 6
- prior_var: float32 [6144], P('col'), may hold values from 0.5 to 2
- incumbent: int32 [1], replicated, may hold values from 0 to 49151
- owner_perm: int32 [6144], P(('row', 'col')), may hold values from 0 to 6143, each once
Outputs:
- panel_result: bfloat16 [49152, 6144], P('row', 'col')
- variance_reduction: float32 [6144], P('col')
- improvement: float32 [6144], P(('row', 'col'))
The draws below stay inside these ranges and needn't reach their ends.
Inputs may be any that keep to these rules, and one draw needn't show every extreme that they name: `diag_inverse`: lower triangular inverses of the factor's diagonal tiles. `owner_perm`: each prediction site once.
All inputs are finite; a program needn't handle non-finite values.
Results may differ from the reference program's by a relative error of at most 0.0064.
Values may be sent and summed in bfloat16 or wider, within the bound.
A program may use at most 192 MiB of HBM per device.

```python
import math
import jax
import jax.numpy as jnp
from jax import lax

B = 1536
RMAX = 384
NT = 32
PRED = 6144


def draw_diag_inverse(key, part):
    key = jax.random.fold_in(key, 11)
    first, second = jax.random.split(key, 2)
    lower = jax.random.normal(first, (2, B, B), jnp.float32) * (0.6 / math.sqrt(B))
    pivots = jax.random.uniform(second, (2, B, 1), jnp.float32, 0.5, 2.0)
    rows = jnp.arange(B)[:, None]
    cols = jnp.arange(B)[None, :]
    matrix = jnp.where(rows > cols, lower, 0.0) + jnp.where(rows == cols, pivots, 0.0)
    return matrix.astype(jnp.bfloat16)


def set_ends(array, own_key, least, top_value):
    dims = array.shape
    spot = [jax.random.randint(jax.random.fold_in(own_key, axis), (), 0, dims[axis]) for axis in range(len(dims))]
    array = array.at[tuple(spot)].set(least)
    longest = dims.index(max(dims))
    spot[longest] = (spot[longest] + 1) % dims[longest]
    return array.at[tuple(spot)].set(top_value)


def levels(key, shape, cuts, least, largest):
    factor_of = 1.0
    for dim, parts in cuts:
        draws = jax.random.uniform(jax.random.fold_in(jax.random.fold_in(key, 6), dim), (parts,), jnp.float32, least / len(cuts), largest / len(cuts))
        factor_of = factor_of * jnp.repeat(jnp.exp(draws), shape[dim] // parts).reshape((-1,) + (1,) * (len(shape) - 1 - dim))
    return factor_of


def gaussian(own_key, dims, spread, reach, cuts=(), held_as=jnp.bfloat16):
    entries = jax.random.normal(own_key, dims, jnp.float32) * spread
    if len(cuts) > 0:
        entries = levels(own_key, dims, cuts, -0.22, 0.18) * entries
    return jnp.clip(entries, min=-reach, max=reach).astype(held_as)


def setup_inputs(seed: int = 0) -> dict:
    key_list = jax.random.split(jax.random.key(seed), 11)
    return {
        "cross_cov": gaussian(key_list[0], (NT * B, PRED), 0.02, 0.15917969, ((0, 32), (1, 4))),
        "diag_inverse": draw_diag_inverse(jax.random.fold_in(key_list[10], 71), 0),
        "factor_u": gaussian(key_list[2], (2, NT * B, RMAX), RMAX ** -0.5, 0.3125, ((1, 32),)),
        "factor_v": gaussian(key_list[3], (2, NT * B, RMAX), B ** -0.5, 0.15625, ((1, 32),)),
        "rank_ids": set_ends(jax.random.randint(key_list[4], (NT, 2), 0, RMAX // 32), jax.random.fold_in(key_list[4], 1), 0, (RMAX // 32) - 1).astype(jnp.int32),
        "weights_obs": gaussian(key_list[5], (2 * B,), 1.0, 6.0, (), jnp.float32),
        "observations": gaussian(key_list[6], (NT * B,), 1.0, 6.0, ((0, 32),), jnp.float32),
        "prior_var": jnp.clip(jnp.exp(math.log(2.0) - 1.3862944 * jax.random.uniform(key_list[7], (PRED,), jnp.float32) ** levels(key_list[7], (PRED,), ((0, 4),), -0.2, 0.2)), 0.5, 2.0),
        "incumbent": jax.random.randint(key_list[8], (1,), 0, NT * B).astype(jnp.int32),
        "owner_perm": jax.random.permutation(key_list[9], PRED).astype(jnp.int32),
    }


def reference(cross_cov, diag_inverse, factor_u, factor_v, rank_ids, weights_obs, observations, prior_var, incumbent, owner_perm):
    tiles = cross_cov.reshape(NT, B, PRED)
    column_ids = jnp.arange(RMAX, dtype=jnp.int32)
    solved = []
    for panel in range(2):
        xsol = jnp.dot(diag_inverse[panel], tiles[panel], preferred_element_type=jnp.float32).astype(jnp.bfloat16)
        solved.append(xsol)
        widths = 32 * (rank_ids[:, panel] + 1)
        lefts = factor_u[panel].reshape(NT, B, RMAX)
        rights = factor_v[panel].reshape(NT, B, RMAX)
        tile_ids = jnp.arange(NT, dtype=jnp.int32)

        def update(packed):
            tile, left, right, width, index = packed
            right = jnp.where(column_ids[None, :] < width, right, jnp.zeros_like(right))
            middle = lax.dot_general(right, xsol, (((0,), (0,)), ((), ())), preferred_element_type=jnp.float32).astype(jnp.bfloat16)
            change = jnp.dot(left, middle, preferred_element_type=jnp.float32)
            fresh = (tile.astype(jnp.float32) - change).astype(jnp.bfloat16)
            keep = jnp.where(index == panel, xsol, tile)
            return jnp.where(index > panel, fresh, keep)
        tiles = lax.map(update, (tiles, lefts, rights, widths, tile_ids))
    stacked = jnp.concatenate(solved, axis=0).astype(jnp.float32)
    reduction = lax.optimization_barrier(jnp.sum(stacked * stacked, axis=0))
    mean = jnp.dot(weights_obs, stacked, precision=lax.Precision.HIGHEST)
    best = observations[incumbent[0]]
    sigma = jnp.sqrt(jnp.maximum(prior_var - reduction, 0.1 * prior_var))
    zscore = (mean - best) / sigma
    density = jnp.exp(-0.5 * zscore * zscore) / jnp.sqrt(2.0 * jnp.pi)
    cumulative = 0.5 * (1.0 + lax.erf(zscore / jnp.sqrt(2.0)))
    scores = sigma * (zscore * cumulative + density)
    return (tiles.reshape(NT * B, PRED), reduction, scores[owner_perm])
```

```python
import jax
import jax.numpy as jnp
from jax import lax
from jax.experimental import pallas as pl
from jax.experimental.pallas import tpu as pltpu
from jax.sharding import PartitionSpec as P

MESH = pl.DeviceIdType.MESH
B = 1536
R = 384
W = 256
NB = 6
Q = 6
KS = B // Q
RC = KS // 4
NS = 2 * NB * Q
SKEW = 6
SLOTS = NS + 5 * SKEW
STAT_AT = 54
SENDS = (33825, 11, 1545, 3584, 112, 135, 1185, 480, 49200, 32805, 33825, 34080, 53248, 45060, 41985, 11520)
DEPTHS = (0, 1753, 2210, 1627, 1739, 2322, 2779, 2196, 1300, 1883, 2340, 1757, 731, 1314, 1771, 1188)
BF = jnp.bfloat16
F32 = jnp.float32


def dot(a, b):
    return jnp.dot(a, b, preferred_element_type=F32)


def lookup(index, table):
    value = jnp.int32(table[0])
    for place in range(1, len(table)):
        value = jnp.where(index == place, jnp.int32(table[place]), value)
    return value


def at0(j):
    return jnp.where(j < 3, j, 2 * j - 2)


def at1(j):
    return jnp.where(j < 3, 2 * j + 3, j + 6)


def solve_kernel(
    cov, dinv, fu, fv, rank, wobs, obs, pvar, inc,
    res, stat,
    xs, ub, vb, vt, db, mb, acc, wv, ov, pv, st, red, mean, bs, rk, ic,
    load, chunk_in, slab_in, tree_out, slab_out, best_in, best_out, stat_in, stat_out, plane_in, plane_out,
):
    myrow = lax.axis_index("row")
    x = lax.axis_index("col")
    z = myrow // 8
    y = (myrow // 2) % 4
    c = myrow % 2
    node = z * 4 + y
    source = node == 0

    def rid(zz, yy, cc):
        return ((zz + 4) % 4) * 8 + ((yy + 4) % 4) * 2 + cc

    around = [rid(z, y + 1, 0), rid(z + 1, y, 0), rid(z, y - 1, 0), rid(z - 1, y, 0)]
    sibling = rid(z, y, 1 - c)
    sends = lookup(node, SENDS)
    depths = lookup(node, DEPTHS)

    barrier = pltpu.get_barrier_semaphore()

    def hello(row, col):
        pl.semaphore_signal(barrier, inc=1, device_id=(row, col), device_id_type=MESH)

    hello(sibling, x)

    @pl.when(c == 0)
    def _():
        for other in around + [rid(z, y + 2, 0), rid(z + 2, y, 0)]:
            hello(other, x)

    @pl.when(jnp.logical_and(c == 1, source))
    def _():
        for dx in range(1, 4):
            hello(myrow, (x + dx) % 4)

    def local(src, dst, place):
        return pltpu.make_async_copy(src, dst, load.at[place])

    def load_cov():
        return local(cov, res, 0)

    def load_d():
        return local(dinv.at[c], db, 1)

    def load_u(p):
        return local(fu.at[p], ub.at[:, pl.ds(p * R, R)], 2 + p)

    def load_v(p):
        return local(fv.at[p], vb.at[p], 4 + p)

    def load_rank():
        return local(rank, rk, 6)

    def load_inc():
        return local(inc, ic, 7)

    def load_obs():
        return local(obs, ov, 8)

    def load_w():
        return local(wobs, wv, 9)

    def load_pv():
        return local(pvar, pv, 10)

    @pl.when(source)
    def _():
        load_cov().start()
        load_d().start()

    load_inc().start()
    load_obs().start()
    load_rank().start()
    for p in range(2):
        load_v(p).start()

    @pl.when(jnp.logical_not(source))
    def _():
        load_cov().start()

    for p in range(2):
        load_u(p).start()
    load_w().start()
    load_pv().start()

    def triangular(k, j):
        cols = pl.ds(pl.multiple_of(j * W, W), W)
        for r in range(B // 256):
            deep = (r + 1) * 256
            xs[k, pl.ds(r * 256, 256), :] = dot(db[pl.ds(r * 256, 256), pl.ds(0, deep)], res[pl.ds(0, deep), cols]).astype(BF)
        res[:, cols] = xs[k]

    def block_copy(k, place):
        return pltpu.make_async_remote_copy(
            xs.at[k], xs.at[k], slab_out.at[place], slab_in.at[k * Q], device_id=(sibling, x), device_id_type=MESH
        )

    def slab_copy(m):
        part = xs.at[m // Q, pl.ds(pl.multiple_of((m % Q) * KS, KS), KS)]
        return pltpu.make_async_remote_copy(
            part, part, slab_out.at[0], slab_in.at[m], device_id=(sibling, x), device_id_type=MESH
        )

    def chunk_copy(i, t, d):
        part = xs.at[i // Q, pl.ds(pl.multiple_of((i % Q) * KS + t * RC, RC), RC)]
        return pltpu.make_async_remote_copy(
            part, part, tree_out.at[t, d], chunk_in.at[i, t], device_id=(around[d], x), device_id_type=MESH
        )

    def drain(sem, blocks):
        part = xs.at[pl.ds(0, blocks)]
        pltpu.make_async_remote_copy(
            part, part, sem, slab_in.at[0], device_id=(sibling, x), device_id_type=MESH
        ).wait_send()

    def best_copy(place, slot, row):
        return pltpu.make_async_remote_copy(
            bs.at[0], bs.at[slot], best_out.at[place], best_in.at[slot], device_id=(row, x), device_id_type=MESH
        )

    def stat_copy(place, row):
        return pltpu.make_async_remote_copy(
            st, st, stat_out.at[place], stat_in, device_id=(row, x), device_id_type=MESH
        )

    @pl.when(jnp.logical_and(source, c == 0))
    def _():
        load_cov().wait()
        load_d().wait()
        triangular(0, 0)

    for p in range(2):
        load_v(p).wait()

    @pl.when(myrow > 0)
    def _():
        for p in range(2):
            for q in range(Q):
                vt[p, q] = vb[p, pl.ds(q * KS, KS), :].T

    load_rank().wait()

    def masked(value, p):
        ids = lax.broadcasted_iota(jnp.int32, value.shape, 0)
        return jnp.where(ids < 32 * (rk[0, p] + 1), value, 0.0).astype(BF)

    @pl.when(c == 0)
    def _():
        pl.semaphore_wait(barrier, 7)

    @pl.when(jnp.logical_and(c == 1, source))
    def _():
        pl.semaphore_wait(barrier, 4)

    @pl.when(jnp.logical_and(c == 1, jnp.logical_not(source)))
    def _():
        pl.semaphore_wait(barrier, 1)

    load_inc().wait()
    load_obs().wait()
    spots = myrow * B + lax.broadcasted_iota(jnp.int32, (12, 128), 0) * 128 + lax.broadcasted_iota(jnp.int32, (12, 128), 1)
    mine = jnp.sum(jnp.where(spots == ic[0], ov[...], 0.0), axis=0, keepdims=True)
    bs[0] = jnp.where(lax.broadcasted_iota(jnp.int32, (8, 128), 0) == 0, mine, 0.0)

    @pl.when(c == 1)
    def _():
        best_copy(0, 1, sibling).start()

    def best_from_sibling():
        best_copy(0, 1, sibling).wait_recv()
        bs[0] = bs[0] + bs[1]

        @pl.when(z > 0)
        def _():
            best_copy(1, 1 + z, rid(0, y, 0)).start()

    def best_over_z():
        for slot in (2, 3, 4):
            best_copy(1, slot, sibling).wait_recv()
        bs[0] = bs[0] + (bs[2] + bs[3] + bs[4])

        @pl.when(y > 0)
        def _():
            best_copy(1, 4 + y, rid(0, 0, 0)).start()

    def best_over_y():
        for slot in (5, 6, 7):
            best_copy(1, slot, sibling).wait_recv()
        bs[0] = bs[0] + (bs[5] + bs[6] + bs[7])
        best_copy(1, 2, sibling).start()

    @pl.when(jnp.logical_and(source, c == 0))
    def _():
        block_copy(0, 0).start()

        def slot(s, carry):
            k = s // Q
            second = jnp.logical_or(k >= 9, jnp.logical_and(k >= 3, k % 2 == 1))

            @pl.when(jnp.logical_and(second, s % Q == 0))
            def _():
                block_copy(k, 0).wait_recv()

            for t in range(4):
                chunk_copy(s, t, t).start()

            @pl.when(jnp.logical_and(s % 2 == 0, s < 10))
            def _():
                j = s // 2 + 1
                triangular(at0(j), j)
                block_copy(at0(j), 0).start()

            @pl.when(s == 10)
            def _():
                best_from_sibling()

            @pl.when(s == 12)
            def _():
                best_over_z()

            @pl.when(s == 14)
            def _():
                best_over_y()

            @pl.when(s == STAT_AT)
            def _():
                stat_copy(0, sibling).wait_recv()
                stat_copy(0, around[0]).start()

            return carry

        lax.fori_loop(0, NS, slot, 0)
        stat_copy(0, sibling).wait_send()
        best_copy(1, 2, sibling).wait_send()
        for t in range(4):
            drain(tree_out.at[t, t], NB // 2)
        drain(slab_out.at[0], NB)
        for p in range(2):
            load_u(p).wait()
        load_w().wait()
        load_pv().wait()

    @pl.when(jnp.logical_and(source, c == 1))
    def _():
        load_cov().wait()
        load_d().wait()
        for p in range(2):
            load_u(p).wait()
        load_w().wait()
        load_pv().wait()
        terms = []
        for p in range(2):
            row = jnp.concatenate([wv[pl.ds(12 * p + g, 1), :] for g in range(12)], axis=1)
            high = row.astype(BF)
            rest = row - high.astype(F32)
            middle = rest.astype(BF)
            low = (rest - middle.astype(F32)).astype(BF)
            ids = lax.broadcasted_iota(jnp.int32, (16, B), 0)
            terms.append(
                jnp.where(
                    ids == 0, high.astype(F32),
                    jnp.where(ids == 1, middle.astype(F32), jnp.where(ids == 2, low.astype(F32), 0.0)),
                ).astype(BF)
            )

        def block(j, carry):
            first, second = at0(j), at1(j)
            cols = pl.ds(pl.multiple_of(j * W, W), W)
            block_copy(first, 0).wait_recv()
            m = dot(vt[0, 0], xs[first, pl.ds(0, KS), :])
            for q in range(1, Q):
                m += dot(vt[0, q], xs[first, pl.ds(q * KS, KS), :])
            mb[0, pl.ds(0, R), :] = masked(m, 0)
            for r in range(B // 256):
                rows = pl.ds(r * 256, 256)
                res[rows, cols] = (res[rows, cols].astype(F32) - dot(ub[rows, pl.ds(0, R)], mb[0, pl.ds(0, R), :])).astype(BF)
            triangular(second, j)
            block_copy(second, 0).start()
            squares = jnp.zeros((8, W), F32)
            total = jnp.zeros((16, W), F32)
            for p, k in ((0, first), (1, second)):
                total += dot(terms[p], xs[k])
                for r in range(B // 256):
                    part = xs[k, pl.ds(r * 256, 256), :].astype(F32)
                    squares += jnp.sum((part * part).reshape(32, 8, W), axis=0)
            line = jnp.sum(squares, axis=0, keepdims=True)
            mline = jnp.sum(total, axis=0, keepdims=True)
            for half in range(2):
                red[pl.ds(2 * j + half, 1), :] = line[:, half * 128 : (half + 1) * 128]
                mean[pl.ds(2 * j + half, 1), :] = mline[:, half * 128 : (half + 1) * 128]
            return carry

        lax.fori_loop(0, NB, block, 0)
        best_copy(1, 2, sibling).wait_recv()
        best = jnp.sum(bs[2])
        prior = pv[...]
        reduction = red[pl.ds(0, 12), :]
        sigma = jnp.sqrt(jnp.maximum(prior - reduction, 0.1 * prior))
        zscore = (mean[pl.ds(0, 12), :] - best) / sigma
        density = jnp.exp(-0.5 * zscore * zscore) / jnp.sqrt(jnp.float32(2.0 * jnp.pi))
        cumulative = 0.5 * (1.0 + lax.erf(zscore / jnp.sqrt(jnp.float32(2.0))))
        st[4, pl.ds(0, 12), :] = reduction
        st[x, pl.ds(0, 12), :] = sigma * (zscore * cumulative + density)

        def plane_copy(dx):
            return pltpu.make_async_remote_copy(
                st.at[x], st.at[x], plane_out.at[dx], plane_in.at[x], device_id=(myrow, (x + dx) % 4), device_id_type=MESH
            )

        for dx in range(1, 4):
            plane_copy(dx).start()
        for dx in range(1, 4):
            other = (x + dx) % 4
            pltpu.make_async_remote_copy(
                st.at[other], st.at[other], plane_out.at[dx], plane_in.at[other],
                device_id=(myrow, other), device_id_type=MESH,
            ).wait_recv()
        stat_copy(0, sibling).start()
        for dx in range(1, 4):
            plane_copy(dx).wait_send()
        stat_copy(0, sibling).wait_send()
        drain(slab_out.at[0], NB)

    @pl.when(jnp.logical_not(source))
    def _():
        longest = jnp.int32(0)
        for t in range(4):
            longest = jnp.maximum(longest, (depths // 8**t) % 8)

        @pl.when(c == 0)
        def _():
            best_from_sibling()

        def sends_on(t, d):
            return (sends // 2 ** (4 * t + d)) % 2 == 1

        load_cov().wait()
        for p in range(2):
            load_u(p).wait()
        load_w().wait()
        load_pv().wait()

        def update(j, first, count):
            rows = pl.ds(pl.multiple_of(first, KS), count)
            cols = pl.ds(pl.multiple_of(j * W, W), W)
            res[rows, cols] = (res[rows, cols].astype(F32) - dot(ub[rows, :], mb[j])).astype(BF)

        def slot(s, carry):
            @pl.when(c == 0)
            def _():
                for t in range(4):
                    i = s - SKEW * ((depths // 8**t) % 8)

                    @pl.when(jnp.logical_and(i >= 0, i < NS))
                    def _():
                        chunk_copy(i, t, 0).wait_recv()
                        for d in range(4):
                            @pl.when(sends_on(t, d))
                            def _():
                                chunk_copy(i, t, d).start()

                    if t == 0:
                        @pl.when(i == STAT_AT)
                        def _():
                            stat_copy(0, sibling).wait_recv()
                            for d in range(4):
                                @pl.when(sends_on(0, d))
                                def _():
                                    stat_copy(d, around[d]).start()
                            stat_copy(4, sibling).start()

            @pl.when(jnp.logical_and(s == 6, jnp.logical_and(c == 0, z == 0)))
            def _():
                best_over_z()

            m = s - SKEW * longest

            @pl.when(jnp.logical_and(m >= 0, m < NS))
            def _():
                @pl.when(c == 0)
                def _():
                    slab_copy(m).start()

                @pl.when(c == 1)
                def _():
                    slab_copy(m).wait_recv()

                k = m // Q
                q = m % Q
                second = jnp.logical_or(k >= 9, jnp.logical_and(k >= 3, k % 2 == 1))
                p = second.astype(jnp.int32)
                j = jnp.where(second, jnp.where(k >= 9, k - 6, (k - 3) // 2), jnp.where(k < 3, k, (k + 2) // 2))
                part = dot(vt[p, q], xs[k, pl.ds(pl.multiple_of(q * KS, KS), KS), :])

                @pl.when(q == 0)
                def _():
                    acc[...] = part

                @pl.when(jnp.logical_and(q > 0, q < Q - 1))
                def _():
                    acc[...] = acc[...] + part

                @pl.when(q == Q - 1)
                def _():
                    mb[j, pl.ds(pl.multiple_of(p * R, R), R), :] = masked(acc[...] + part, p)

                before = k - 1
                was = jnp.logical_or(before >= 9, jnp.logical_and(before >= 3, before % 2 == 1))

                @pl.when(was)
                def _():
                    update(jnp.where(before >= 9, before - 6, (before - 3) // 2), q * KS, KS)

            return carry

        lax.fori_loop(0, SLOTS, slot, 0)

        def last(q, carry):
            update(NB - 1, q * KS, KS)
            return carry

        lax.fori_loop(0, Q, last, 0)

        @pl.when(c == 0)
        def _():
            drain(slab_out.at[0], 2 * NB)
            stat_copy(4, sibling).wait_send()
            for d in range(4):
                @pl.when(sends_on(0, d))
                def _():
                    stat_copy(d, around[d]).wait_send()
                for t in range(4):
                    @pl.when(sends_on(t, d))
                    def _():
                        drain(tree_out.at[t, d], NB // 2)

            @pl.when(jnp.logical_or(z > 0, y > 0))
            def _():
                best_copy(1, 2, sibling).wait_send()

        @pl.when(c == 1)
        def _():
            stat_copy(0, sibling).wait_recv()

    @pl.when(c == 1)
    def _():
        best_copy(0, 1, sibling).wait_send()

    stat[...] = st[...]


def place_kernel(res, stat, perm, out, var, imp, lines, slots, sems):
    whole = pltpu.make_async_copy(res, out, sems.at[0])
    whole.start()
    scores = pltpu.make_async_copy(stat, lines, sems.at[1])
    scores.start()
    owners = pltpu.make_async_copy(perm, slots, sems.at[2])
    owners.start()
    var[...] = stat[4, pl.ds(0, 12), :]
    scores.wait()
    owners.wait()

    def pick(i, carry):
        site = slots[i]
        imp[i] = lines[site // B, (site % B) // 128, site % 128]
        return carry

    lax.fori_loop(0, imp.shape[0], pick, 0)
    whole.wait()


def shards(cross_cov, diag_inverse, factor_u, factor_v, rank_ids, weights_obs, observations, prior_var, incumbent, owner_perm):
    hbm = pl.BlockSpec(memory_space=pl.ANY)
    vmem = pl.BlockSpec(memory_space=pltpu.VMEM)
    dma = pltpu.SemaphoreType.DMA
    solved, stats = pl.pallas_call(
        solve_kernel,
        name="solve",
        out_shape=(pltpu.VMEM((B, B), BF), pltpu.VMEM((5, 16, 128), F32)),
        in_specs=[hbm] * 9,
        out_specs=(vmem, vmem),
        scratch_shapes=[
            pltpu.VMEM((2 * NB, B, W), BF),
            pltpu.VMEM((B, 2 * R), BF),
            pltpu.VMEM((2, B, R), BF),
            pltpu.VMEM((2, Q, R, KS), BF),
            pltpu.VMEM((B, B), BF),
            pltpu.VMEM((NB, 2 * R, W), BF),
            pltpu.VMEM((R, W), F32),
            pltpu.VMEM((24, 128), F32),
            pltpu.VMEM((12, 128), F32),
            pltpu.VMEM((12, 128), F32),
            pltpu.VMEM((5, 16, 128), F32),
            pltpu.VMEM((16, 128), F32),
            pltpu.VMEM((16, 128), F32),
            pltpu.VMEM((8, 8, 128), F32),
            pltpu.SMEM((1, 2), jnp.int32),
            pltpu.SMEM((1,), jnp.int32),
            dma((11,)),
            dma((NS, 4)),
            dma((NS,)),
            dma((4, 4)),
            dma((1,)),
            dma((8,)),
            dma((2,)),
            dma,
            dma((5,)),
            dma((4,)),
            dma((4,)),
        ],
        compiler_params=pltpu.CompilerParams(collective_id=0, has_side_effects=True, vmem_limit_bytes=48 << 20),
        cost_estimate=pl.CostEstimate(flops=7_250_000_000, bytes_accessed=9_400_000, transcendentals=0),
    )(
        cross_cov, diag_inverse, factor_u, factor_v, rank_ids, weights_obs.reshape(24, 128),
        observations.reshape(12, 128), prior_var.reshape(12, 128), incumbent,
    )
    slots = owner_perm.shape[0]
    result, reduction, improvement = pl.pallas_call(
        place_kernel,
        name="place",
        out_shape=(
            jax.ShapeDtypeStruct((B, B), BF),
            jax.ShapeDtypeStruct((12, 128), F32),
            jax.ShapeDtypeStruct((slots,), F32),
        ),
        in_specs=[vmem, vmem, hbm],
        out_specs=(hbm, vmem, pl.BlockSpec(memory_space=pltpu.SMEM)),
        scratch_shapes=[pltpu.SMEM((5, 16, 128), F32), pltpu.SMEM((slots,), jnp.int32), dma((3,))],
        compiler_params=pltpu.CompilerParams(vmem_limit_bytes=16 << 20),
    )(solved, stats, owner_perm)
    return result, reduction.reshape(B), improvement


def solution(mesh):
    placed = (
        P("row", "col"), P(), P(None, "row", None), P(None, "row", None), P("row", None),
        P(), P("row"), P("col"), P(), P(("row", "col")),
    )
    return jax.shard_map(
        shards, mesh=mesh, in_specs=placed, out_specs=(P("row", "col"), P("col"), P(("row", "col"))), check_vma=False
    )
```

```python
import functools
import jax
import jax.numpy as jnp
from jax import lax
from jax.experimental import pallas as pl
from jax.experimental.pallas import tpu as pltpu
from jax.sharding import PartitionSpec as P

MESH = pl.DeviceIdType.MESH
B = 1536
R = 384
W = 256
NB = 6
Q = 2
KS = B // Q
RC = KS // 4
NS = 2 * NB * Q
AHEAD = 6
STAT_AT = NS - 1
UPDATE_AT = {2: (0, 1), 3: (1, 2), 4: (1, 3), 6: (2, 4)}[Q]
PLACES = (0, 0, 4, 2, 1, 8, 12, 9, 5, 15, 16, 13, 3, 11, 14, 10)
ROLES = (
    ((1, (0, 1, 3)), (3, ()), (3, ()), (3, ())),
    ((2, (0, 3)), (4, ()), (2, (1, 2)), (4, ())),
    ((2, (0, 1, 2)), (2, (3,)), (4, ()), (4, ())),
    ((3, (0,)), (3, (1, 3)), (3, (2,)), (5, ())),
    ((4, (0,)), (4, (1,)), (4, (2,)), (4, (3,))),
)
EARLY = tuple(AHEAD if any(not children for _, children in role) else 0 for role in ROLES)
LEADS = tuple(EARLY[place // 4] if ROLES[place // 4][-place % 4][1] else 0 for place in PLACES)
FIRST = tuple(sum(1 << (d + place) % 4 for d in ROLES[place // 4][-place % 4][1]) for place in PLACES)
BF = jnp.bfloat16
F32 = jnp.float32


def dot(a, b):
    return jnp.dot(a, b, preferred_element_type=F32)


def lookup(index, table):
    value = jnp.int32(table[0])
    for place in range(1, len(table)):
        value = jnp.where(index == place, jnp.int32(table[place]), value)
    return value


def pick(index, values):
    value = values[0]
    for place in range(1, len(values)):
        value = jnp.where(index == place, values[place], value)
    return value


def at0(j):
    return j


def at1(j):
    return NB + j


def solve_kernel(
    cov, dinv, fu, fv, rank, wobs, obs, pvar, inc,
    res, stat,
    xs, ub, vb, vt, db, mb, acc, wv, ov, pv, st, own, theirs, bs, rk, ic,
    load, chunk_in, slab_in, tree_out, slab_out, best_in, best_out, stat_in, stat_out, plane_in, plane_out,
):
    myrow = lax.axis_index("row")
    x = lax.axis_index("col")
    z = myrow // 8
    y = (myrow // 2) % 4
    c = myrow % 2
    node = z * 4 + y
    source = node == 0

    def rid(zz, yy, cc):
        return ((zz + 4) % 4) * 8 + ((yy + 4) % 4) * 2 + cc

    hub = (c == 0) == source

    def hub_of(zz, yy):
        first = jnp.logical_and((zz + 4) % 4 == 0, (yy + 4) % 4 == 0)
        return rid(zz, yy, jnp.where(first, 0, 1))

    around = [hub_of(z, y + 1), hub_of(z + 1, y), hub_of(z, y - 1), hub_of(z - 1, y)]
    sibling = rid(z, y, 1 - c)
    place = lookup(node, PLACES)
    role = place // 4
    turns = place % 4

    barrier = pltpu.get_barrier_semaphore()

    def hello(row, col):
        pl.semaphore_signal(barrier, inc=1, device_id=(row, col), device_id_type=MESH)

    hello(sibling, x)

    @pl.when(hub)
    def _():
        for other in around + [hub_of(z, y + 2), hub_of(z + 2, y)]:
            hello(other, x)

    @pl.when(jnp.logical_and(c == 1, source))
    def _():
        for dx in range(1, 4):
            hello(myrow, (x + dx) % 4)

    def local(src, dst, place):
        return pltpu.make_async_copy(src, dst, load.at[place])

    def load_cov():
        return local(cov, res, 0)

    def load_cov_block(j):
        cols = pl.ds(j * W, W)
        return local(cov.at[:, cols], res.at[:, cols], 11 + j)

    def load_d(r):
        part = (pl.ds(r * W, W), pl.ds(0, (r + 1) * W))
        return local(dinv.at[(c, *part)], db.at[part], 17 + r)

    def load_u(p):
        return local(fu.at[p], ub.at[:, pl.ds(p * R, R)], 2 + p)

    def load_v(p):
        return local(fv.at[p], vb.at[p], 4 + p)

    def load_rank():
        return local(rank, rk, 6)

    def load_inc():
        return local(inc, ic, 7)

    def load_obs():
        return local(obs, ov, 8)

    def load_w():
        return local(wobs, wv, 9)

    def load_pv():
        return local(pvar, pv, 10)

    @pl.when(source)
    def _():
        load_cov_block(0).start()
        for r in range(NB):
            load_d(r).start()

    load_inc().start()
    load_obs().start()

    @pl.when(myrow > 0)
    def _():
        load_rank().start()
        for p in range(2):
            load_v(p).start()

    @pl.when(source)
    def _():
        for j in range(1, NB):
            load_cov_block(j).start()

    @pl.when(jnp.logical_not(source))
    def _():
        load_cov().start()

    @pl.when(myrow > 0)
    def _():
        for p in range(2):
            load_u(p).start()

    @pl.when(source)
    def _():
        load_w().start()

    @pl.when(myrow == 1)
    def _():
        load_pv().start()

    def block_rows(k, first=0, count=B):
        return pl.ds(pl.multiple_of(k * B + first, 128), count)

    def triangular(k, j):
        cols = pl.ds(pl.multiple_of(j * W, W), W)
        for r in range(NB):
            deep = (r + 1) * W
            xs[block_rows(k, r * W, W), :] = dot(db[pl.ds(r * W, W), pl.ds(0, deep)], res[pl.ds(0, deep), cols]).astype(BF)
        res[:, cols] = xs[block_rows(k), :]

    def block_copy(k, place):
        part = xs.at[block_rows(k)]
        return pltpu.make_async_remote_copy(
            part, part, slab_out.at[place], slab_in.at[k * Q], device_id=(sibling, x), device_id_type=MESH
        )

    def slab_copy(m):
        part = xs.at[pl.ds(pl.multiple_of(m * KS, KS), KS)]
        return pltpu.make_async_remote_copy(
            part, part, slab_out.at[0], slab_in.at[m], device_id=(sibling, x), device_id_type=MESH
        )

    def chunk_copy(i, t, d):
        part = xs.at[pl.ds(pl.multiple_of(i * KS + t * RC, RC), RC)]
        return pltpu.make_async_remote_copy(
            part, part, tree_out.at[t, d], chunk_in.at[i * 4 + t], device_id=(around[d], x), device_id_type=MESH
        )

    def drain(sem, blocks):
        part = xs.at[pl.ds(0, blocks * B)]
        pltpu.make_async_remote_copy(
            part, part, sem, slab_in.at[0], device_id=(sibling, x), device_id_type=MESH
        ).wait_send()

    def best_copy(place, slot, row):
        return pltpu.make_async_remote_copy(
            bs.at[0], bs.at[slot], best_out.at[place], best_in.at[slot], device_id=(row, x), device_id_type=MESH
        )

    def stat_copy(place, row):
        return pltpu.make_async_remote_copy(
            st, st, stat_out.at[place], stat_in, device_id=(row, x), device_id_type=MESH
        )

    @pl.when(source)
    def _():
        load_cov_block(0).wait()
        for r in range(NB):
            load_d(r).wait()

    @pl.when(myrow == 0)
    def _():
        triangular(0, 0)

    @pl.when(myrow > 0)
    def _():
        for p in range(2):
            load_v(p).wait()
            vt[p] = vb[p].T
        load_rank().wait()

    def masked(value, p):
        ids = lax.broadcasted_iota(jnp.int32, value.shape, 0)
        return jnp.where(ids < 32 * (rk[0, p] + 1), value, 0.0).astype(BF)

    @pl.when(hub)
    def _():
        pl.semaphore_wait(barrier, 7)

    @pl.when(jnp.logical_and(c == 1, source))
    def _():
        pl.semaphore_wait(barrier, 4)

    @pl.when(jnp.logical_and(c == 0, jnp.logical_not(source)))
    def _():
        pl.semaphore_wait(barrier, 1)

    load_inc().wait()
    load_obs().wait()
    spots = myrow * B + lax.broadcasted_iota(jnp.int32, (12, 128), 0) * 128 + lax.broadcasted_iota(jnp.int32, (12, 128), 1)
    mine = jnp.sum(jnp.where(spots == ic[0], ov[...], 0.0), axis=0, keepdims=True)
    bs[0] = jnp.where(lax.broadcasted_iota(jnp.int32, (8, 128), 0) == 0, mine, 0.0)

    @pl.when(jnp.logical_not(hub))
    def _():
        best_copy(0, 1, sibling).start()

    def best_from_sibling():
        best_copy(0, 1, sibling).wait_recv()
        bs[0] = bs[0] + bs[1]

        @pl.when(z > 0)
        def _():
            best_copy(1, 1 + z, hub_of(0, y)).start()

    def best_over_z():
        for slot in (2, 3, 4):
            best_copy(1, slot, sibling).wait_recv()
        bs[0] = bs[0] + (bs[2] + bs[3] + bs[4])

        @pl.when(y > 0)
        def _():
            best_copy(1, 4 + y, hub_of(0, 0)).start()

    def best_over_y():
        for slot in (5, 6, 7):
            best_copy(1, slot, sibling).wait_recv()
        bs[0] = bs[0] + (bs[5] + bs[6] + bs[7])
        best_copy(1, 2, sibling).start()

    def weights(p):
        row = jnp.concatenate([wv[pl.ds(12 * p + g, 1), :] for g in range(12)], axis=1)
        high = row.astype(BF).astype(F32)
        middle = (row - high).astype(BF).astype(F32)
        low = row - high - middle
        ids = lax.broadcasted_iota(jnp.int32, (16, B), 0)
        return jnp.where(ids == 0, high, jnp.where(ids == 1, middle, jnp.where(ids == 2, low, 0.0))).astype(BF)

    def tally(k, j, terms):
        squares = jnp.zeros((8, W), F32)
        for r in range(NB):
            part = xs[block_rows(k, r * W, W), :].astype(F32)
            squares += jnp.sum((part * part).reshape(W // 8, 8, W), axis=0)
        line = jnp.sum(squares, axis=0, keepdims=True)
        mline = jnp.sum(dot(terms, xs[block_rows(k), :]), axis=0, keepdims=True)
        for half in range(2):
            own[0, pl.ds(2 * j + half, 1), :] = line[:, half * 128 : (half + 1) * 128]
            own[1, pl.ds(2 * j + half, 1), :] = mline[:, half * 128 : (half + 1) * 128]

    def sums_copy():
        return pltpu.make_async_remote_copy(
            own, theirs, best_out.at[2], best_in.at[0], device_id=(sibling, x), device_id_type=MESH
        )

    @pl.when(jnp.logical_and(source, c == 0))
    def _():
        block_copy(0, 0).start()
        for j in range(1, NB):
            load_cov_block(j).wait()
        load_w().wait()
        terms = weights(0)

        def slot(s, carry):
            k = s // Q

            @pl.when(jnp.logical_and(k >= NB, s % Q == 0))
            def _():
                block_copy(k, 0).wait_recv()

            for t in range(4):
                chunk_copy(s, t, t).start()

            @pl.when(jnp.logical_and(s % 2 == 0, s < 10))
            def _():
                j = s // 2 + 1
                triangular(at0(j), j)
                block_copy(at0(j), 0).start()

            @pl.when(s == 6 * Q)
            def _():
                best_from_sibling()

            @pl.when(s == 6 * Q + 1)
            def _():
                best_over_z()

            @pl.when(s == 7 * Q)
            def _():
                best_over_y()

            after = s - 4 * Q

            @pl.when(jnp.logical_and(jnp.logical_and(after >= 0, after < 12), after % 2 == 0))
            def _():
                tally(at0(after // 2), after // 2, terms)

            @pl.when(after == 11)
            def _():
                sums_copy().start()

            @pl.when(s == STAT_AT)
            def _():
                stat_copy(0, sibling).wait_recv()
                stat_copy(0, around[0]).start()

            return carry

        lax.fori_loop(0, NS, slot, 0)
        sums_copy().wait_send()
        stat_copy(0, sibling).wait_send()
        best_copy(1, 2, sibling).wait_send()
        for t in range(4):
            drain(tree_out.at[t, t], NB // 2)
        drain(slab_out.at[0], NB)

    @pl.when(jnp.logical_and(source, c == 1))
    def _():
        for j in range(1, NB):
            load_cov_block(j).wait()
        for p in range(2):
            load_u(p).wait()
        load_w().wait()
        load_pv().wait()
        terms = weights(1)

        def block(j, carry):
            first, second = at0(j), at1(j)
            cols = pl.ds(pl.multiple_of(j * W, W), W)
            block_copy(first, 0).wait_recv()
            mb[0, pl.ds(0, R), :] = masked(dot(vt[0], xs[block_rows(first), :]), 0)
            res[:, cols] = (res[:, cols].astype(F32) - dot(ub[:, pl.ds(0, R)], mb[0, pl.ds(0, R), :])).astype(BF)
            triangular(second, j)
            block_copy(second, 0).start()
            tally(second, j, terms)
            return carry

        lax.fori_loop(0, NB, block, 0)
        best_copy(1, 2, sibling).wait_recv()
        best = jnp.sum(bs[2])
        prior = pv[...]
        sums_copy().wait_recv()
        reduction = own[0, pl.ds(0, 12), :] + theirs[0, pl.ds(0, 12), :]
        mean = own[1, pl.ds(0, 12), :] + theirs[1, pl.ds(0, 12), :]
        sigma = jnp.sqrt(jnp.maximum(prior - reduction, 0.1 * prior))
        zscore = (mean - best) / sigma
        density = jnp.exp(-0.5 * zscore * zscore) / jnp.sqrt(jnp.float32(2.0 * jnp.pi))
        cumulative = 0.5 * (1.0 + lax.erf(zscore / jnp.sqrt(jnp.float32(2.0))))
        st[4, pl.ds(0, 12), :] = reduction
        st[x, pl.ds(0, 12), :] = sigma * (zscore * cumulative + density)

        def plane_copy(dx):
            return pltpu.make_async_remote_copy(
                st.at[x], st.at[x], plane_out.at[dx], plane_in.at[x], device_id=(myrow, (x + dx) % 4), device_id_type=MESH
            )

        for dx in range(1, 4):
            plane_copy(dx).start()
        for dx in range(1, 4):
            other = (x + dx) % 4
            pltpu.make_async_remote_copy(
                st.at[other], st.at[other], plane_out.at[dx], plane_in.at[other],
                device_id=(myrow, other), device_id_type=MESH,
            ).wait_recv()
        stat_copy(0, sibling).start()
        for dx in range(1, 4):
            plane_copy(dx).wait_send()
        stat_copy(0, sibling).wait_send()
        drain(slab_out.at[0], NB)

    @pl.when(jnp.logical_not(source))
    def _():
        turned = [(turns + d) % 4 for d in range(4)]
        beside = [pick(turned[d], around) for d in range(4)]
        rows_of = [turned[t] * RC for t in range(4)]

        @pl.when(hub)
        def _():
            best_from_sibling()

        load_cov().wait()
        for p in range(2):
            load_u(p).wait()

        def role_chunk(m, t, lead, d=0):
            part = xs.at[pl.ds(pl.multiple_of(m * KS + (lead * KS + rows_of[t]), RC), RC)]
            return pltpu.make_async_remote_copy(
                part, part, tree_out.at[t, d], chunk_in.at[m * 4 + (lead * 4 + turned[t])],
                device_id=(beside[d], x), device_id_type=MESH,
            )

        def send_on(m, number):
            for t, (_, children) in enumerate(ROLES[number]):
                if children:
                    role_chunk(m, t, EARLY[number]).wait_recv()
                    for d in children:
                        role_chunk(m, t, EARLY[number], d).start()

        def take(m, number):
            for t, (_, children) in enumerate(ROLES[number]):
                if not children:
                    role_chunk(m, t, 0).wait_recv()

        stat_slot = STAT_AT - lookup(node, LEADS)

        def stat_sends(act):
            for d in range(4):
                pl.when(jnp.bitwise_and(lookup(node, FIRST), 1 << d) != 0)(functools.partial(act, d))

        lead = lookup(role, EARLY)

        def forward(m):
            @pl.when(jnp.logical_and(m >= -lead, m < NS - lead))
            def _():
                for number in range(len(ROLES)):
                    pl.when(role == number)(functools.partial(send_on, m, number))

            @pl.when(m >= 0)
            def _():
                for number in range(len(ROLES)):
                    if EARLY[number]:
                        pl.when(role == number)(functools.partial(take, m, number))

            @pl.when(m == stat_slot)
            def _():
                stat_copy(0, sibling).wait_recv()
                stat_sends(lambda d: stat_copy(d, around[d]).start())
                stat_copy(4, sibling).start()

            @pl.when(jnp.logical_and(m == 3 - AHEAD, z == 0))
            def _():
                best_over_z()

        def middle(k, p, j):
            mb[j, pl.ds(pl.multiple_of(p * R, R), R), :] = masked(dot(vt[p], xs[block_rows(k), :]), p)

        def update(j, first, count):
            rows = pl.ds(first, count)
            cols = pl.ds(pl.multiple_of(j * W, W), W)
            res[rows, cols] = (res[rows, cols].astype(F32) - dot(ub[rows, :], mb[j])).astype(BF)

        def block(step, carry):
            k = step - AHEAD // Q
            before = jnp.maximum(k - 1, 0)
            second = before >= NB
            p = second.astype(jnp.int32)
            j = before - NB * p

            def slab(q, carry):
                m = k * Q + q

                @pl.when(hub)
                def _():
                    forward(m)

                    @pl.when(k >= 0)
                    def _():
                        slab_copy(m).start()

                @pl.when(jnp.logical_and(jnp.logical_not(hub), k >= 0))
                def _():
                    slab_copy(m).wait_recv()

                @pl.when(jnp.logical_and(q == 0, k > 0))
                def _():
                    middle(before, p, j)

                for piece in range(2):
                    @pl.when(jnp.logical_and(q == UPDATE_AT[piece], second))
                    def _():
                        update(j, piece * (B // 2), B // 2)

                @pl.when(jnp.logical_and(q == Q - 1, k == 2 * NB - 1))
                def _():
                    acc[...] = dot(vt[1, :, pl.ds(0, B // 2)], xs[block_rows(k, 0, B // 2), :])

                return carry

            return lax.fori_loop(0, Q, slab, carry)

        lax.fori_loop(0, 2 * NB + AHEAD // Q, block, 0)
        rest = dot(vt[1, :, pl.ds(B // 2, B // 2)], xs[block_rows(2 * NB - 1, B // 2, B // 2), :])
        mb[NB - 1, pl.ds(R, R), :] = masked(acc[...] + rest, 1)
        update(NB - 1, 0, B)

        @pl.when(hub)
        def _():
            drain(slab_out.at[0], 2 * NB)
            stat_copy(4, sibling).wait_send()
            stat_sends(lambda d: stat_copy(d, around[d]).wait_send())
            for number, trees in enumerate(ROLES):
                @pl.when(role == number)
                def _():
                    for t, (_, children) in enumerate(trees):
                        for d in children:
                            drain(tree_out.at[t, d], NB // 2)

            @pl.when(jnp.logical_or(z > 0, y > 0))
            def _():
                best_copy(1, 2, sibling).wait_send()

        @pl.when(jnp.logical_not(hub))
        def _():
            stat_copy(0, sibling).wait_recv()

    @pl.when(jnp.logical_not(hub))
    def _():
        best_copy(0, 1, sibling).wait_send()

    stat[...] = st[...]


def place_kernel(res, stat, perm, out, var, imp, lines, slots, sems):
    whole = pltpu.make_async_copy(res, out, sems.at[0])
    whole.start()
    scores = pltpu.make_async_copy(stat, lines, sems.at[1])
    scores.start()
    owners = pltpu.make_async_copy(perm, slots, sems.at[2])
    owners.start()
    var[...] = stat[4, pl.ds(0, 12), :]
    scores.wait()
    owners.wait()

    def pick(i, carry):
        site = slots[i]
        imp[i] = lines[site // B, (site % B) // 128, site % 128]
        return carry

    lax.fori_loop(0, imp.shape[0], pick, 0)
    whole.wait()


def shards(cross_cov, diag_inverse, factor_u, factor_v, rank_ids, weights_obs, observations, prior_var, incumbent, owner_perm):
    hbm = pl.BlockSpec(memory_space=pltpu.HBM)
    vmem = pl.BlockSpec(memory_space=pltpu.VMEM)
    dma = pltpu.SemaphoreType.DMA
    solved, stats = pl.pallas_call(
        solve_kernel,
        name="solve",
        out_shape=(pltpu.VMEM((B, B), BF), pltpu.VMEM((5, 16, 128), F32)),
        in_specs=[hbm] * 9,
        out_specs=(vmem, vmem),
        scratch_shapes=[
            pltpu.VMEM((2 * NB * B, W), BF),
            pltpu.VMEM((B, 2 * R), BF),
            pltpu.VMEM((2, B, R), BF),
            pltpu.VMEM((2, R, B), BF),
            pltpu.VMEM((B, B), BF),
            pltpu.VMEM((NB, 2 * R, W), BF),
            pltpu.VMEM((R, W), F32),
            pltpu.VMEM((24, 128), F32),
            pltpu.VMEM((12, 128), F32),
            pltpu.VMEM((12, 128), F32),
            pltpu.VMEM((5, 16, 128), F32),
            pltpu.VMEM((2, 16, 128), F32),
            pltpu.VMEM((2, 16, 128), F32),
            pltpu.VMEM((8, 8, 128), F32),
            pltpu.SMEM((1, 2), jnp.int32),
            pltpu.SMEM((1,), jnp.int32),
            dma((23,)),
            dma((NS * 4,)),
            dma((NS,)),
            dma((4, 4)),
            dma((1,)),
            dma((8,)),
            dma((3,)),
            dma,
            dma((5,)),
            dma((4,)),
            dma((4,)),
        ],
        compiler_params=pltpu.CompilerParams(collective_id=0, has_side_effects=True, vmem_limit_bytes=48 << 20),
        cost_estimate=pl.CostEstimate(flops=7_250_000_000, bytes_accessed=9_400_000, transcendentals=0),
    )(
        *(
            pltpu.with_memory_space_constraint(array, pltpu.HBM)
            for array in (
                cross_cov, diag_inverse, factor_u, factor_v, rank_ids, weights_obs.reshape(24, 128),
                observations.reshape(12, 128), prior_var.reshape(12, 128),
            )
        ),
        incumbent,
    )
    slots = owner_perm.shape[0]
    result, reduction, improvement = pl.pallas_call(
        place_kernel,
        name="place",
        out_shape=(
            jax.ShapeDtypeStruct((B, B), BF),
            jax.ShapeDtypeStruct((12, 128), F32),
            jax.ShapeDtypeStruct((slots,), F32),
        ),
        in_specs=[vmem, vmem, hbm],
        out_specs=(hbm, vmem, pl.BlockSpec(memory_space=pltpu.SMEM)),
        scratch_shapes=[pltpu.SMEM((5, 16, 128), F32), pltpu.SMEM((slots,), jnp.int32), dma((3,))],
        compiler_params=pltpu.CompilerParams(vmem_limit_bytes=16 << 20),
    )(solved, stats, pltpu.with_memory_space_constraint(owner_perm, pltpu.HBM))
    return result, reduction.reshape(B), improvement


def solution(mesh):
    placed = (
        P("row", "col"), P(), P(None, "row", None), P(None, "row", None), P("row", None),
        P(), P("row"), P("col"), P(), P(("row", "col")),
    )
    return jax.shard_map(
        shards, mesh=mesh, in_specs=placed, out_specs=(P("row", "col"), P("col"), P(("row", "col"))), check_vma=False
    )
```

```python
import functools
import jax
import jax.numpy as jnp
from jax import lax
from jax.experimental import pallas as pl
from jax.experimental.pallas import tpu as pltpu
from jax.sharding import PartitionSpec as P

MESH = pl.DeviceIdType.MESH
B = 1536
R = 384
W = 256
NB = 6
NS = 4 * NB
HALF = B // 2
RC = HALF // 4
AHEAD = 7
STAT_AT = NS - 1
PLACES = (0, 0, 4, 2, 1, 8, 12, 9, 5, 15, 16, 13, 3, 11, 14, 10)
ROLES = (
    ((1, (0, 1, 3)), (3, ()), (3, ()), (3, ())),
    ((2, (0, 3)), (4, ()), (2, (1, 2)), (4, ())),
    ((2, (0, 1, 2)), (2, (3,)), (4, ()), (4, ())),
    ((3, (0,)), (3, (1, 3)), (3, (2,)), (5, ())),
    ((4, (0,)), (4, (1,)), (4, (2,)), (4, (3,))),
)
EARLY = tuple(AHEAD if any(not children for _, children in role) else 0 for role in ROLES)
LEADS = tuple(EARLY[place // 4] if ROLES[place // 4][-place % 4][1] else 0 for place in PLACES)
FIRST = tuple(sum(1 << (d + place) % 4 for d in ROLES[place // 4][-place % 4][1]) for place in PLACES)
PARTS = 4
BF = jnp.bfloat16
F32 = jnp.float32


def dot(a, b):
    return jnp.dot(a, b, preferred_element_type=F32)


def lookup(index, table):
    value = jnp.int32(table[0])
    for place in range(1, len(table)):
        value = jnp.where(index == place, jnp.int32(table[place]), value)
    return value


def pick(index, values):
    value = values[0]
    for place in range(1, len(values)):
        value = jnp.where(index == place, values[place], value)
    return value


def at0(j):
    return j


def at1(j):
    return NB + j


def solve_kernel(
    cov, dinv, fu, fv, rank, wobs, obs, pvar, inc,
    res, stat,
    xs, ub, vb, vt, db, mb, acc, wv, ov, pv, st, own, theirs, bs, rk, ic,
    load, chunk_in, slab_in, tree_out, slab_out, best_in, best_out, stat_in, stat_out, plane_in, plane_out,
):
    myrow = lax.axis_index("row")
    x = lax.axis_index("col")
    z = myrow // 8
    y = (myrow // 2) % 4
    c = myrow % 2
    node = z * 4 + y
    source = node == 0

    def rid(zz, yy, cc):
        return ((zz + 4) % 4) * 8 + ((yy + 4) % 4) * 2 + cc

    hub = (c == 0) == source

    def hub_of(zz, yy):
        first = jnp.logical_and((zz + 4) % 4 == 0, (yy + 4) % 4 == 0)
        return rid(zz, yy, jnp.where(first, 0, 1))

    around = [hub_of(z, y + 1), hub_of(z + 1, y), hub_of(z, y - 1), hub_of(z - 1, y)]
    sibling = rid(z, y, 1 - c)
    place = lookup(node, PLACES)
    role = place // 4
    turns = place % 4

    barrier = pltpu.get_barrier_semaphore()

    def hello(row, col):
        pl.semaphore_signal(barrier, inc=1, device_id=(row, col), device_id_type=MESH)

    hello(sibling, x)

    @pl.when(hub)
    def _():
        for other in around + [hub_of(z, y + 2), hub_of(z + 2, y)]:
            hello(other, x)

    @pl.when(jnp.logical_and(c == 1, source))
    def _():
        for dx in range(1, 4):
            hello(myrow, (x + dx) % 4)

    def local(src, dst, place):
        return pltpu.make_async_copy(src, dst, load.at[place])

    def load_cov():
        return local(cov, res, 0)

    def load_cov_block(j):
        cols = pl.ds(j * W, W)
        return local(cov.at[:, cols], res.at[:, cols], 11 + j)

    def load_d(r):
        part = (pl.ds(r * W, W), pl.ds(0, (r + 1) * W))
        return local(dinv.at[(c, *part)], db.at[part], 17 + r)

    def load_u(p):
        return local(fu.at[p], ub.at[p], 2 + p)

    def load_v(p):
        return local(fv.at[p], vb.at[p], 4 + p)

    def load_rank():
        return local(rank, rk, 6)

    def load_inc():
        return local(inc, ic, 7)

    def load_obs():
        return local(obs, ov, 8)

    def load_w():
        return local(wobs, wv, 9)

    def load_pv():
        return local(pvar, pv, 10)

    @pl.when(source)
    def _():
        load_cov_block(0).start()
        for r in range(NB):
            load_d(r).start()

    load_inc().start()
    load_obs().start()

    @pl.when(myrow > 0)
    def _():
        load_rank().start()
        for p in range(2):
            load_v(p).start()

    @pl.when(source)
    def _():
        for j in range(1, NB):
            load_cov_block(j).start()

    @pl.when(jnp.logical_not(source))
    def _():
        load_cov().start()

    @pl.when(myrow > 0)
    def _():
        for p in range(2):
            load_u(p).start()

    @pl.when(source)
    def _():
        load_w().start()

    @pl.when(myrow == 1)
    def _():
        load_pv().start()

    def block_rows(k, first=0, count=B):
        return pl.ds(pl.multiple_of(k * B + first, 128), count)

    def triangular(k, j, blocks=range(NB)):
        cols = pl.ds(pl.multiple_of(j * W, W), W)
        for r in blocks:
            deep = (r + 1) * W
            xs[block_rows(k, r * W, W), :] = dot(db[pl.ds(r * W, W), pl.ds(0, deep)], res[pl.ds(0, deep), cols]).astype(BF)
        if blocks[-1] == NB - 1:
            res[:, cols] = xs[block_rows(k), :]

    def block_copy(k, place):
        part = xs.at[block_rows(k)]
        return pltpu.make_async_remote_copy(
            part, part, slab_out.at[place], slab_in.at[k], device_id=(sibling, x), device_id_type=MESH
        )

    def slab_copy(m):
        part = xs.at[pl.ds(pl.multiple_of(m * HALF, HALF), HALF)]
        return pltpu.make_async_remote_copy(
            part, part, slab_out.at[0], slab_in.at[m], device_id=(sibling, x), device_id_type=MESH
        )

    def chunk_copy(i, t):
        part = xs.at[pl.ds(pl.multiple_of(i * HALF + t * RC, RC), RC)]
        return pltpu.make_async_remote_copy(
            part, part, tree_out.at[t, t], chunk_in.at[i * 4 + t], device_id=(around[t], x), device_id_type=MESH
        )

    def drain(sem, blocks):
        part = xs.at[pl.ds(0, blocks * B)]
        pltpu.make_async_remote_copy(
            part, part, sem, slab_in.at[0], device_id=(sibling, x), device_id_type=MESH
        ).wait_send()

    def best_copy(place, slot, row):
        return pltpu.make_async_remote_copy(
            bs.at[0], bs.at[slot], best_out.at[place], best_in.at[slot], device_id=(row, x), device_id_type=MESH
        )

    def stat_copy(place, row):
        return pltpu.make_async_remote_copy(
            st, st, stat_out.at[place], stat_in, device_id=(row, x), device_id_type=MESH
        )

    @pl.when(source)
    def _():
        load_cov_block(0).wait()
        for r in range(NB // 2):
            load_d(r).wait()

    @pl.when(myrow == 0)
    def _():
        triangular(0, 0, range(NB // 2))

    @pl.when(myrow > 0)
    def _():
        for p in range(2):
            load_v(p).wait()
            vt[p] = vb[p].T
        load_rank().wait()

    def masked(value, p):
        ids = lax.broadcasted_iota(jnp.int32, value.shape, 0)
        return jnp.where(ids < 32 * (rk[0, p] + 1), value, 0.0).astype(BF)

    @pl.when(hub)
    def _():
        pl.semaphore_wait(barrier, 7)

    @pl.when(jnp.logical_and(c == 1, source))
    def _():
        pl.semaphore_wait(barrier, 4)

    @pl.when(jnp.logical_and(c == 0, jnp.logical_not(source)))
    def _():
        pl.semaphore_wait(barrier, 1)

    load_inc().wait()
    load_obs().wait()
    spots = myrow * B + lax.broadcasted_iota(jnp.int32, (12, 128), 0) * 128 + lax.broadcasted_iota(jnp.int32, (12, 128), 1)
    mine = jnp.sum(jnp.where(spots == ic[0], ov[...], 0.0), axis=0, keepdims=True)
    bs[0] = jnp.where(lax.broadcasted_iota(jnp.int32, (8, 128), 0) == 0, mine, 0.0)

    @pl.when(jnp.logical_not(hub))
    def _():
        best_copy(0, 1, sibling).start()

    def best_from_sibling():
        best_copy(0, 1, sibling).wait_recv()
        bs[0] = bs[0] + bs[1]

        @pl.when(z > 0)
        def _():
            best_copy(1, 1 + z, hub_of(0, y)).start()

    def best_over_z():
        for slot in (2, 3, 4):
            best_copy(1, slot, sibling).wait_recv()
        bs[0] = bs[0] + (bs[2] + bs[3] + bs[4])

        @pl.when(y > 0)
        def _():
            best_copy(1, 4 + y, hub_of(0, 0)).start()

    def best_over_y():
        for slot in (5, 6, 7):
            best_copy(1, slot, sibling).wait_recv()
        bs[0] = bs[0] + (bs[5] + bs[6] + bs[7])
        best_copy(1, 2, sibling).start()

    def weights(p):
        row = jnp.concatenate([wv[pl.ds(12 * p + g, 1), :] for g in range(12)], axis=1)
        high = row.astype(BF).astype(F32)
        middle = (row - high).astype(BF).astype(F32)
        low = row - high - middle
        ids = lax.broadcasted_iota(jnp.int32, (16, B), 0)
        return jnp.where(ids == 0, high, jnp.where(ids == 1, middle, jnp.where(ids == 2, low, 0.0))).astype(BF)

    def tally(k, j, terms):
        squares = jnp.zeros((8, W), F32)
        for r in range(NB):
            part = xs[block_rows(k, r * W, W), :].astype(F32)
            squares += jnp.sum((part * part).reshape(W // 8, 8, W), axis=0)
        line = jnp.sum(squares, axis=0, keepdims=True)
        mline = jnp.sum(dot(terms, xs[block_rows(k), :]), axis=0, keepdims=True)
        for half in range(2):
            own[0, pl.ds(2 * j + half, 1), :] = line[:, half * 128 : (half + 1) * 128]
            own[1, pl.ds(2 * j + half, 1), :] = mline[:, half * 128 : (half + 1) * 128]

    def sums_copy():
        return pltpu.make_async_remote_copy(
            own, theirs, best_out.at[2], best_in.at[0], device_id=(sibling, x), device_id_type=MESH
        )

    @pl.when(jnp.logical_and(source, c == 0))
    def _():
        load_w().wait()
        terms = weights(0)

        def slot(s, carry):
            k = s // 2

            @pl.when(jnp.logical_and(k >= NB, s % 2 == 0))
            def _():
                block_copy(k, 0).wait_recv()

            for t in range(4):
                chunk_copy(s, t).start()

            @pl.when(s == 0)
            def _():
                for r in range(NB // 2, NB):
                    load_d(r).wait()
                triangular(0, 0, range(NB // 2, NB))
                block_copy(0, 0).start()
                for j in range(1, NB):
                    load_cov_block(j).wait()

            @pl.when(jnp.logical_and(s % 2 == 1, s < 10))
            def _():
                j = (s + 1) // 2
                triangular(at0(j), j)
                block_copy(at0(j), 0).start()

            @pl.when(s == 12)
            def _():
                best_from_sibling()

            @pl.when(s == 13)
            def _():
                best_over_z()

            @pl.when(s == 14)
            def _():
                best_over_y()

            after = s - 8

            @pl.when(jnp.logical_and(jnp.logical_and(after >= 0, after < 12), after % 2 == 0))
            def _():
                tally(at0(after // 2), after // 2, terms)

            @pl.when(after == 11)
            def _():
                sums_copy().start()

            @pl.when(s == STAT_AT)
            def _():
                stat_copy(0, sibling).wait_recv()
                stat_copy(0, around[0]).start()

            return carry

        lax.fori_loop(0, NS, slot, 0)
        sums_copy().wait_send()
        stat_copy(0, sibling).wait_send()
        best_copy(1, 2, sibling).wait_send()
        for t in range(4):
            drain(tree_out.at[t, t], NB // 2)
        drain(slab_out.at[0], NB)

    @pl.when(jnp.logical_and(source, c == 1))
    def _():
        for r in range(NB // 2, NB):
            load_d(r).wait()
        for j in range(1, NB):
            load_cov_block(j).wait()
        for p in range(2):
            load_u(p).wait()
        load_w().wait()
        load_pv().wait()
        terms = weights(1)

        def block(j, carry):
            first, second = at0(j), at1(j)
            cols = pl.ds(pl.multiple_of(j * W, W), W)
            block_copy(first, 0).wait_recv()
            mb[...] = masked(dot(vt[0], xs[block_rows(first), :]), 0)
            res[:, cols] = (res[:, cols].astype(F32) - dot(ub[0], mb[...])).astype(BF)
            triangular(second, j)
            block_copy(second, 0).start()
            tally(second, j, terms)
            return carry

        lax.fori_loop(0, NB, block, 0)
        best_copy(1, 2, sibling).wait_recv()
        best = jnp.sum(bs[2])
        prior = pv[...]
        sums_copy().wait_recv()
        reduction = own[0, pl.ds(0, 12), :] + theirs[0, pl.ds(0, 12), :]
        mean = own[1, pl.ds(0, 12), :] + theirs[1, pl.ds(0, 12), :]
        sigma = jnp.sqrt(jnp.maximum(prior - reduction, 0.1 * prior))
        zscore = (mean - best) / sigma
        density = jnp.exp(-0.5 * zscore * zscore) / jnp.sqrt(jnp.float32(2.0 * jnp.pi))
        cumulative = 0.5 * (1.0 + lax.erf(zscore / jnp.sqrt(jnp.float32(2.0))))
        st[4, pl.ds(0, 12), :] = reduction
        st[x, pl.ds(0, 12), :] = sigma * (zscore * cumulative + density)

        def plane_copy(dx):
            return pltpu.make_async_remote_copy(
                st.at[x], st.at[x], plane_out.at[dx], plane_in.at[x], device_id=(myrow, (x + dx) % 4), device_id_type=MESH
            )

        for dx in range(1, 4):
            plane_copy(dx).start()
        for dx in range(1, 4):
            other = (x + dx) % 4
            pltpu.make_async_remote_copy(
                st.at[other], st.at[other], plane_out.at[dx], plane_in.at[other],
                device_id=(myrow, other), device_id_type=MESH,
            ).wait_recv()
        stat_copy(0, sibling).start()
        for dx in range(1, 4):
            plane_copy(dx).wait_send()
        stat_copy(0, sibling).wait_send()
        drain(slab_out.at[0], NB)

    @pl.when(jnp.logical_not(source))
    def _():
        turned = [(turns + d) % 4 for d in range(4)]
        beside = [pick(turned[d], around) for d in range(4)]
        rows_of = [turned[t] * RC for t in range(4)]

        @pl.when(hub)
        def _():
            best_from_sibling()

        load_cov().wait()
        for p in range(2):
            load_u(p).wait()

        def role_rows(i, t):
            return xs.at[pl.ds(pl.multiple_of(i * HALF + rows_of[t], RC), RC)]

        def role_chunk(i, t, d=0):
            part = role_rows(i, t)
            return pltpu.make_async_remote_copy(
                part, part, tree_out.at[t, d], chunk_in.at[i * 4 + turned[t]], device_id=(beside[d], x), device_id_type=MESH
            )

        def send_on(i, number):
            for t, (_, children) in enumerate(ROLES[number]):
                if children:
                    role_chunk(i, t).wait_recv()
                    for d in children:
                        role_chunk(i, t, d).start()

        def take(i, number):
            for t, (_, children) in enumerate(ROLES[number]):
                if not children:
                    role_chunk(i, t).wait_recv()

        def take_last(number):
            for leaf in (False, True):
                for t, (_, children) in enumerate(ROLES[number]):
                    if leaf == (not children):
                        if leaf:
                            role_chunk(NS - 1, t).wait_recv()
                        part = role_rows(NS - 1, t)
                        pltpu.make_async_remote_copy(
                            part, part, slab_out.at[0], slab_in.at[NS - 1], device_id=(sibling, x), device_id_type=MESH
                        ).start()

        stat_slot = STAT_AT - lookup(node, LEADS)

        def stat_sends(act):
            for d in range(4):
                pl.when(jnp.bitwise_and(lookup(node, FIRST), 1 << d) != 0)(functools.partial(act, d))

        lead = lookup(role, EARLY)

        def forward(m):
            i = m + lead

            @pl.when(jnp.logical_and(i >= 0, i < NS))
            def _():
                for number in range(len(ROLES)):
                    pl.when(role == number)(functools.partial(send_on, i, number))

            @pl.when(jnp.logical_and(m >= 0, m < NS - 1))
            def _():
                for number in range(len(ROLES)):
                    if EARLY[number]:
                        pl.when(role == number)(functools.partial(take, m, number))
                slab_copy(m).start()

            @pl.when(m == NS - 1)
            def _():
                for number in range(len(ROLES)):
                    pl.when(role == number)(functools.partial(take_last, number))

            @pl.when(m == stat_slot)
            def _():
                stat_copy(0, sibling).wait_recv()
                stat_sends(lambda d: stat_copy(d, around[d]).start())
                stat_copy(4, sibling).start()

            @pl.when(jnp.logical_and(m == 3 - AHEAD, z == 0))
            def _():
                best_over_z()

        def middle(k, p):
            mb[...] = masked(dot(vt[p], xs[block_rows(k), :]), p)

        def update(p, j, first, count):
            rows = pl.ds(first, count)
            cols = pl.ds(pl.multiple_of(j * W, W), W)
            res[rows, cols] = (res[rows, cols].astype(F32) - dot(ub[p, rows, :], mb[...])).astype(BF)

        def slot(step, carry):
            m = step - AHEAD
            k = jnp.maximum(m, 0) // 2
            q = jnp.maximum(m, 0) % 2
            before = jnp.maximum(k - 1, 0)
            p = (before >= NB).astype(jnp.int32)
            j = before - NB * p

            @pl.when(hub)
            def _():
                forward(m)

            @pl.when(jnp.logical_and(jnp.logical_not(hub), m >= 0))
            def _():
                slab_copy(m).wait_recv()

            @pl.when(jnp.logical_and(q == 0, jnp.logical_and(k > 0, m > 0)))
            def _():
                middle(before, p)

            for piece in range(2):
                @pl.when(jnp.logical_and(q == piece, k > 0))
                def _():
                    update(p, j, piece * HALF, HALF)

            @pl.when(m == NS - 2)
            def _():
                acc[...] = dot(vt[1, :, pl.ds(0, B - HALF)], xs[block_rows(2 * NB - 1, 0, B - HALF), :])

            return carry

        lax.fori_loop(0, NS + AHEAD, slot, 0)
        rest = dot(vt[1, :, pl.ds(B - HALF, HALF)], xs[block_rows(2 * NB - 1, B - HALF, HALF), :])
        mb[...] = masked(acc[...] + rest, 1)
        update(1, NB - 1, 0, B)

        @pl.when(hub)
        def _():
            drain(slab_out.at[0], 2 * NB)
            stat_copy(4, sibling).wait_send()
            stat_sends(lambda d: stat_copy(d, around[d]).wait_send())
            for number, trees in enumerate(ROLES):
                @pl.when(role == number)
                def _():
                    for t, (_, children) in enumerate(trees):
                        for d in children:
                            drain(tree_out.at[t, d], NB // 2)

            @pl.when(jnp.logical_or(z > 0, y > 0))
            def _():
                best_copy(1, 2, sibling).wait_send()

        @pl.when(jnp.logical_not(hub))
        def _():
            stat_copy(0, sibling).wait_recv()

    @pl.when(jnp.logical_not(hub))
    def _():
        best_copy(0, 1, sibling).wait_send()

    stat[...] = st[...]


def place_kernel(res, stat, perm, out, var, imp, lines, slots, sems):
    scores = pltpu.make_async_copy(stat.at[pl.ds(0, 4)], lines, sems.at[PARTS])
    scores.start()
    owners = pltpu.make_async_copy(perm, slots, sems.at[PARTS + 1])
    owners.start()
    step = B // PARTS
    parts = [pltpu.make_async_copy(res.at[pl.ds(r * step, step)], out.at[pl.ds(r * step, step)], sems.at[r]) for r in range(PARTS)]
    for part in parts:
        part.start()
    var[...] = stat[4, pl.ds(0, 12), :]
    scores.wait()
    owners.wait()
    for i in range(imp.shape[0]):
        site = slots[i]
        line = lax.shift_right_logical(site, 7)
        plane = lax.shift_right_logical(line * 43, 9)
        imp[i] = lines[plane, line - 12 * plane, jnp.bitwise_and(site, 127)]
    for part in parts:
        part.wait()


def shards(cross_cov, diag_inverse, factor_u, factor_v, rank_ids, weights_obs, observations, prior_var, incumbent, owner_perm):
    hbm = pl.BlockSpec(memory_space=pltpu.HBM)
    vmem = pl.BlockSpec(memory_space=pltpu.VMEM)
    dma = pltpu.SemaphoreType.DMA
    solved, stats = pl.pallas_call(
        solve_kernel,
        name="solve",
        out_shape=(pltpu.VMEM((B, B), BF), pltpu.VMEM((5, 16, 128), F32)),
        in_specs=[hbm] * 9,
        out_specs=(vmem, vmem),
        scratch_shapes=[
            pltpu.VMEM((2 * NB * B, W), BF),
            pltpu.VMEM((2, B, R), BF),
            pltpu.VMEM((2, B, R), BF),
            pltpu.VMEM((2, R, B), BF),
            pltpu.VMEM((B, B), BF),
            pltpu.VMEM((R, W), BF),
            pltpu.VMEM((R, W), F32),
            pltpu.VMEM((24, 128), F32),
            pltpu.VMEM((12, 128), F32),
            pltpu.VMEM((12, 128), F32),
            pltpu.VMEM((5, 16, 128), F32),
            pltpu.VMEM((2, 16, 128), F32),
            pltpu.VMEM((2, 16, 128), F32),
            pltpu.VMEM((8, 8, 128), F32),
            pltpu.SMEM((1, 2), jnp.int32),
            pltpu.SMEM((1,), jnp.int32),
            dma((23,)),
            dma((NS * 4,)),
            dma((NS,)),
            dma((4, 4)),
            dma((1,)),
            dma((8,)),
            dma((3,)),
            dma,
            dma((5,)),
            dma((4,)),
            dma((4,)),
        ],
        compiler_params=pltpu.CompilerParams(collective_id=0, has_side_effects=True, vmem_limit_bytes=48 << 20),
        cost_estimate=pl.CostEstimate(flops=7_250_000_000, bytes_accessed=9_400_000, transcendentals=0),
    )(
        *(
            pltpu.with_memory_space_constraint(array, pltpu.HBM)
            for array in (
                cross_cov, diag_inverse, factor_u, factor_v, rank_ids, weights_obs.reshape(24, 128),
                observations.reshape(12, 128), prior_var.reshape(12, 128),
            )
        ),
        incumbent,
    )
    slots = owner_perm.shape[0]
    result, reduction, improvement = pl.pallas_call(
        place_kernel,
        name="place",
        out_shape=(
            jax.ShapeDtypeStruct((B, B), BF),
            jax.ShapeDtypeStruct((12, 128), F32),
            jax.ShapeDtypeStruct((slots,), F32),
        ),
        in_specs=[vmem, vmem, hbm],
        out_specs=(hbm, vmem, pl.BlockSpec(memory_space=pltpu.SMEM)),
        scratch_shapes=[pltpu.SMEM((4, 16, 128), F32), pltpu.SMEM((slots,), jnp.int32), dma((PARTS + 2,))],
        compiler_params=pltpu.CompilerParams(vmem_limit_bytes=16 << 20),
    )(solved, stats, pltpu.with_memory_space_constraint(owner_perm, pltpu.HBM))
    return result, reduction.reshape(B), improvement


def solution(mesh):
    placed = (
        P("row", "col"), P(), P(None, "row", None), P(None, "row", None), P("row", None),
        P(), P("row"), P("col"), P(), P(("row", "col")),
    )
    return jax.shard_map(
        shards, mesh=mesh, in_specs=placed, out_specs=(P("row", "col"), P("col"), P(("row", "col"))), check_vma=False
    )
```

```python
import functools
import jax
import jax.numpy as jnp
from jax import lax
from jax.experimental import pallas as pl
from jax.experimental.pallas import tpu as pltpu
from jax.sharding import PartitionSpec as P

MESH = pl.DeviceIdType.MESH
B = 1536
R = 384
W = 256
NB = 6
NS = 4 * NB
HALF = B // 2
RC = HALF // 4
AHEAD = 7
STAT_AT = NS - 1
PLACES = (0, 0, 4, 2, 1, 8, 12, 9, 5, 15, 16, 13, 3, 11, 14, 10)
ROLES = (
    ((1, (0, 1, 3)), (3, ()), (3, ()), (3, ())),
    ((2, (0, 3)), (4, ()), (2, (1, 2)), (4, ())),
    ((2, (0, 1, 2)), (2, (3,)), (4, ()), (4, ())),
    ((3, (0,)), (3, (1, 3)), (3, (2,)), (5, ())),
    ((4, (0,)), (4, (1,)), (4, (2,)), (4, (3,))),
)
EARLY = tuple(AHEAD if any(not children for _, children in role) else 0 for role in ROLES)
LEADS = tuple(EARLY[place // 4] if ROLES[place // 4][-place % 4][1] else 0 for place in PLACES)
FIRST = tuple(sum(1 << (d + place) % 4 for d in ROLES[place // 4][-place % 4][1]) for place in PLACES)
PARTS = 4
BF = jnp.bfloat16
F32 = jnp.float32


def dot(a, b):
    return jnp.dot(a, b, preferred_element_type=F32)


def lookup(index, table):
    value = jnp.int32(table[0])
    for place in range(1, len(table)):
        value = jnp.where(index == place, jnp.int32(table[place]), value)
    return value


def pick(index, values):
    value = values[0]
    for place in range(1, len(values)):
        value = jnp.where(index == place, values[place], value)
    return value


def at0(j):
    return j


def at1(j):
    return NB + j


def solve_kernel(
    cov, dinv, fu, fv, rank, wobs, obs, pvar, inc,
    res, stat,
    xs, ub, vb, vt, db, mb, acc, wv, ov, pv, st, own, theirs, bs, rk, ic,
    load, chunk_in, slab_in, tree_out, slab_out, best_in, best_out, stat_in, stat_out, plane_in, plane_out,
):
    myrow = lax.axis_index("row")
    x = lax.axis_index("col")
    z = myrow // 8
    y = (myrow // 2) % 4
    c = myrow % 2
    node = z * 4 + y
    source = node == 0

    def rid(zz, yy, cc):
        return ((zz + 4) % 4) * 8 + ((yy + 4) % 4) * 2 + cc

    hub = (c == 0) == source

    def hub_of(zz, yy):
        first = jnp.logical_and((zz + 4) % 4 == 0, (yy + 4) % 4 == 0)
        return rid(zz, yy, jnp.where(first, 0, 1))

    around = [hub_of(z, y + 1), hub_of(z + 1, y), hub_of(z, y - 1), hub_of(z - 1, y)]
    sibling = rid(z, y, 1 - c)
    place = lookup(node, PLACES)
    role = place // 4
    turns = place % 4

    barrier = pltpu.get_barrier_semaphore()

    def hello(row, col):
        pl.semaphore_signal(barrier, inc=1, device_id=(row, col), device_id_type=MESH)

    hello(sibling, x)

    @pl.when(hub)
    def _():
        for other in around + [hub_of(z, y + 2), hub_of(z + 2, y)]:
            hello(other, x)

    @pl.when(jnp.logical_and(c == 1, source))
    def _():
        for dx in range(1, 4):
            hello(myrow, (x + dx) % 4)

    def local(src, dst, place):
        return pltpu.make_async_copy(src, dst, load.at[place])

    def load_cov():
        return local(cov, res, 0)

    def load_cov_block(j):
        cols = pl.ds(pl.multiple_of(j * W, W), W)
        return local(cov.at[:, cols], res.at[:, cols], 11 + j)

    def load_d(r):
        part = (pl.ds(r * W, W), pl.ds(0, (r + 1) * W))
        return local(dinv.at[(c, *part)], db.at[part], 17 + r)

    def load_u(p):
        return local(fu.at[p], ub.at[p], 2 + p)

    def load_v(p):
        return local(fv.at[p], vb.at[p], 4 + p)

    def load_rank():
        return local(rank, rk, 6)

    def load_inc():
        return local(inc, ic, 7)

    def load_obs():
        return local(obs, ov, 8)

    def load_w():
        return local(wobs, wv, 9)

    def load_pv():
        return local(pvar, pv, 10)

    @pl.when(source)
    def _():
        load_cov_block(0).start()
        for r in range(NB):
            load_d(r).start()

    load_inc().start()
    load_obs().start()

    @pl.when(myrow > 0)
    def _():
        load_rank().start()
        for p in range(2):
            load_v(p).start()

    @pl.when(source)
    def _():
        for j in range(1, NB):
            load_cov_block(j).start()

    @pl.when(jnp.logical_not(source))
    def _():
        load_cov().start()

    @pl.when(myrow > 0)
    def _():
        for p in range(2):
            load_u(p).start()

    @pl.when(source)
    def _():
        load_w().start()

    @pl.when(myrow == 1)
    def _():
        load_pv().start()

    def block_rows(k, first=0, count=B):
        return pl.ds(pl.multiple_of(k * B + first, 128), count)

    def triangular(k, j, blocks=range(NB)):
        cols = pl.ds(pl.multiple_of(j * W, W), W)
        for r in blocks:
            deep = (r + 1) * W
            xs[block_rows(k, r * W, W), :] = dot(db[pl.ds(r * W, W), pl.ds(0, deep)], res[pl.ds(0, deep), cols]).astype(BF)
        if blocks[-1] == NB - 1:
            res[:, cols] = xs[block_rows(k), :]

    def block_copy(k, place):
        part = xs.at[block_rows(k)]
        return pltpu.make_async_remote_copy(
            part, part, slab_out.at[place], slab_in.at[k], device_id=(sibling, x), device_id_type=MESH
        )

    def slab_copy(m):
        part = xs.at[pl.ds(pl.multiple_of(m * HALF, HALF), HALF)]
        return pltpu.make_async_remote_copy(
            part, part, slab_out.at[0], slab_in.at[m], device_id=(sibling, x), device_id_type=MESH
        )

    def chunk_copy(i, t):
        part = xs.at[pl.ds(pl.multiple_of(i * HALF + t * RC, RC), RC)]
        return pltpu.make_async_remote_copy(
            part, part, tree_out.at[t, t], chunk_in.at[i * 4 + t], device_id=(around[t], x), device_id_type=MESH
        )

    def drain(sem, blocks):
        part = xs.at[pl.ds(0, blocks * B)]
        pltpu.make_async_remote_copy(
            part, part, sem, slab_in.at[0], device_id=(sibling, x), device_id_type=MESH
        ).wait_send()

    def best_copy(place, slot, row):
        return pltpu.make_async_remote_copy(
            bs.at[0], bs.at[slot], best_out.at[place], best_in.at[slot], device_id=(row, x), device_id_type=MESH
        )

    def stat_copy(place, row):
        return pltpu.make_async_remote_copy(
            st, st, stat_out.at[place], stat_in, device_id=(row, x), device_id_type=MESH
        )

    @pl.when(source)
    def _():
        load_cov_block(0).wait()
        for r in range(NB // 2):
            load_d(r).wait()

    @pl.when(myrow == 0)
    def _():
        triangular(0, 0, range(NB // 2))

    @pl.when(myrow > 0)
    def _():
        for p in range(2):
            load_v(p).wait()
            vt[p] = vb[p].T
        load_rank().wait()

    def masked(value, p):
        ids = lax.broadcasted_iota(jnp.int32, value.shape, 0)
        return jnp.where(ids < 32 * (rk[0, p] + 1), value, 0.0).astype(BF)

    @pl.when(hub)
    def _():
        pl.semaphore_wait(barrier, 7)

    @pl.when(jnp.logical_and(c == 1, source))
    def _():
        pl.semaphore_wait(barrier, 4)

    @pl.when(jnp.logical_and(c == 0, jnp.logical_not(source)))
    def _():
        pl.semaphore_wait(barrier, 1)

    load_inc().wait()
    load_obs().wait()
    spots = myrow * B + lax.broadcasted_iota(jnp.int32, (12, 128), 0) * 128 + lax.broadcasted_iota(jnp.int32, (12, 128), 1)
    mine = jnp.sum(jnp.where(spots == ic[0], ov[...], 0.0), axis=0, keepdims=True)
    bs[0] = jnp.where(lax.broadcasted_iota(jnp.int32, (8, 128), 0) == 0, mine, 0.0)

    @pl.when(jnp.logical_not(hub))
    def _():
        best_copy(0, 1, sibling).start()

    def best_from_sibling():
        best_copy(0, 1, sibling).wait_recv()
        bs[0] = bs[0] + bs[1]

        @pl.when(z > 0)
        def _():
            best_copy(1, 1 + z, hub_of(0, y)).start()

    def best_over_z():
        for slot in (2, 3, 4):
            best_copy(1, slot, sibling).wait_recv()
        bs[0] = bs[0] + (bs[2] + bs[3] + bs[4])

        @pl.when(y > 0)
        def _():
            best_copy(1, 4 + y, hub_of(0, 0)).start()

    def best_over_y():
        for slot in (5, 6, 7):
            best_copy(1, slot, sibling).wait_recv()
        bs[0] = bs[0] + (bs[5] + bs[6] + bs[7])
        best_copy(1, 2, sibling).start()

    def weights(p):
        row = jnp.concatenate([wv[pl.ds(12 * p + g, 1), :] for g in range(12)], axis=1)
        high = row.astype(BF).astype(F32)
        middle = (row - high).astype(BF).astype(F32)
        low = row - high - middle
        ids = lax.broadcasted_iota(jnp.int32, (16, B), 0)
        return jnp.where(ids == 0, high, jnp.where(ids == 1, middle, jnp.where(ids == 2, low, 0.0))).astype(BF)

    def tally(k, j, terms):
        squares = jnp.zeros((8, W), F32)
        for r in range(NB):
            part = xs[block_rows(k, r * W, W), :].astype(F32)
            squares += jnp.sum((part * part).reshape(W // 8, 8, W), axis=0)
        line = jnp.sum(squares, axis=0, keepdims=True)
        mline = jnp.sum(dot(terms, xs[block_rows(k), :]), axis=0, keepdims=True)
        for half in range(2):
            own[0, pl.ds(2 * j + half, 1), :] = line[:, half * 128 : (half + 1) * 128]
            own[1, pl.ds(2 * j + half, 1), :] = mline[:, half * 128 : (half + 1) * 128]

    def sums_copy():
        return pltpu.make_async_remote_copy(
            own, theirs, best_out.at[2], best_in.at[0], device_id=(sibling, x), device_id_type=MESH
        )

    @pl.when(jnp.logical_and(source, c == 0))
    def _():
        load_w().wait()
        terms = weights(0)

        def slot(s, carry):
            k = s // 2

            @pl.when(jnp.logical_and(k >= NB, s % 2 == 0))
            def _():
                block_copy(k, 0).wait_recv()

            for t in range(4):
                chunk_copy(s, t).start()

            @pl.when(s == 0)
            def _():
                for r in range(NB // 2, NB):
                    load_d(r).wait()
                triangular(0, 0, range(NB // 2, NB))
                block_copy(0, 0).start()

            @pl.when(jnp.logical_and(s % 2 == 1, s < 10))
            def _():
                j = (s + 1) // 2
                load_cov_block(j).wait()
                triangular(at0(j), j)
                block_copy(at0(j), 0).start()

            @pl.when(s == 12)
            def _():
                best_from_sibling()

            @pl.when(s == 13)
            def _():
                best_over_z()

            @pl.when(s == 14)
            def _():
                best_over_y()

            after = s - 8

            @pl.when(jnp.logical_and(jnp.logical_and(after >= 0, after < 12), after % 2 == 0))
            def _():
                tally(at0(after // 2), after // 2, terms)

            @pl.when(after == 11)
            def _():
                sums_copy().start()

            @pl.when(s == STAT_AT)
            def _():
                stat_copy(0, sibling).wait_recv()
                stat_copy(0, around[0]).start()

            return carry

        lax.fori_loop(0, NS, slot, 0)
        sums_copy().wait_send()
        stat_copy(0, sibling).wait_send()
        best_copy(1, 2, sibling).wait_send()
        for t in range(4):
            drain(tree_out.at[t, t], NB // 2)
        drain(slab_out.at[0], NB)

    @pl.when(jnp.logical_and(source, c == 1))
    def _():
        for r in range(NB // 2, NB):
            load_d(r).wait()
        for j in range(1, NB):
            load_cov_block(j).wait()
        for p in range(2):
            load_u(p).wait()
        load_w().wait()
        load_pv().wait()
        terms = weights(1)

        def block(j, carry):
            first, second = at0(j), at1(j)
            cols = pl.ds(pl.multiple_of(j * W, W), W)
            block_copy(first, 0).wait_recv()
            mb[...] = masked(dot(vt[0], xs[block_rows(first), :]), 0)
            res[:, cols] = (res[:, cols].astype(F32) - dot(ub[0], mb[...])).astype(BF)
            triangular(second, j)
            block_copy(second, 0).start()
            tally(second, j, terms)
            return carry

        lax.fori_loop(0, NB, block, 0)
        best_copy(1, 2, sibling).wait_recv()
        best = jnp.sum(bs[2])
        prior = pv[...]
        sums_copy().wait_recv()
        reduction = own[0, pl.ds(0, 12), :] + theirs[0, pl.ds(0, 12), :]
        mean = own[1, pl.ds(0, 12), :] + theirs[1, pl.ds(0, 12), :]
        sigma = jnp.sqrt(jnp.maximum(prior - reduction, 0.1 * prior))
        zscore = (mean - best) / sigma
        density = jnp.exp(-0.5 * zscore * zscore) / jnp.sqrt(jnp.float32(2.0 * jnp.pi))
        cumulative = 0.5 * (1.0 + lax.erf(zscore / jnp.sqrt(jnp.float32(2.0))))
        st[4, pl.ds(0, 12), :] = reduction
        st[x, pl.ds(0, 12), :] = sigma * (zscore * cumulative + density)

        def plane_copy(dx):
            return pltpu.make_async_remote_copy(
                st.at[x], st.at[x], plane_out.at[dx], plane_in.at[x], device_id=(myrow, (x + dx) % 4), device_id_type=MESH
            )

        for dx in range(1, 4):
            plane_copy(dx).start()
        for dx in range(1, 4):
            other = (x + dx) % 4
            pltpu.make_async_remote_copy(
                st.at[other], st.at[other], plane_out.at[dx], plane_in.at[other],
                device_id=(myrow, other), device_id_type=MESH,
            ).wait_recv()
        stat_copy(0, sibling).start()
        for dx in range(1, 4):
            plane_copy(dx).wait_send()
        stat_copy(0, sibling).wait_send()
        drain(slab_out.at[0], NB)

    @pl.when(jnp.logical_not(source))
    def _():
        turned = [(turns + d) % 4 for d in range(4)]
        beside = [pick(turned[d], around) for d in range(4)]
        rows_of = [turned[t] * RC for t in range(4)]

        @pl.when(hub)
        def _():
            best_from_sibling()

        load_cov().wait()
        for p in range(2):
            load_u(p).wait()

        def role_rows(i, t):
            return xs.at[pl.ds(pl.multiple_of(i * HALF + rows_of[t], RC), RC)]

        def role_chunk(i, t, d=0):
            part = role_rows(i, t)
            return pltpu.make_async_remote_copy(
                part, part, tree_out.at[t, d], chunk_in.at[i * 4 + turned[t]], device_id=(beside[d], x), device_id_type=MESH
            )

        def send_on(i, number):
            for t, (_, children) in enumerate(ROLES[number]):
                if children:
                    role_chunk(i, t).wait_recv()
                    for d in children:
                        role_chunk(i, t, d).start()

        def take(i, number):
            for t, (_, children) in enumerate(ROLES[number]):
                if not children:
                    role_chunk(i, t).wait_recv()

        def take_last(number):
            for leaf in (False, True):
                for t, (_, children) in enumerate(ROLES[number]):
                    if leaf == (not children):
                        if leaf:
                            role_chunk(NS - 1, t).wait_recv()
                        part = role_rows(NS - 1, t)
                        pltpu.make_async_remote_copy(
                            part, part, slab_out.at[0], slab_in.at[NS - 1], device_id=(sibling, x), device_id_type=MESH
                        ).start()

        stat_slot = STAT_AT - lookup(node, LEADS)

        def stat_sends(act):
            for d in range(4):
                pl.when(jnp.bitwise_and(lookup(node, FIRST), 1 << d) != 0)(functools.partial(act, d))

        lead = lookup(role, EARLY)

        def forward(m):
            i = m + lead

            @pl.when(jnp.logical_and(i >= 0, i < NS))
            def _():
                for number in range(len(ROLES)):
                    pl.when(role == number)(functools.partial(send_on, i, number))

            @pl.when(jnp.logical_and(m >= 0, m < NS - 1))
            def _():
                for number in range(len(ROLES)):
                    if EARLY[number]:
                        pl.when(role == number)(functools.partial(take, m, number))
                slab_copy(m).start()

            @pl.when(m == NS - 1)
            def _():
                for number in range(len(ROLES)):
                    pl.when(role == number)(functools.partial(take_last, number))

            @pl.when(m == stat_slot)
            def _():
                stat_copy(0, sibling).wait_recv()
                stat_sends(lambda d: stat_copy(d, around[d]).start())
                stat_copy(4, sibling).start()

            @pl.when(jnp.logical_and(m == 3 - AHEAD, z == 0))
            def _():
                best_over_z()

        def middle(k, p):
            mb[...] = masked(dot(vt[p], xs[block_rows(k), :]), p)

        def update(p, j, first, count):
            rows = pl.ds(first, count)
            cols = pl.ds(pl.multiple_of(j * W, W), W)
            res[rows, cols] = (res[rows, cols].astype(F32) - dot(ub[p, rows, :], mb[...])).astype(BF)

        def slot(step, carry):
            m = step - AHEAD
            k = jnp.maximum(m, 0) // 2
            q = jnp.maximum(m, 0) % 2
            before = jnp.maximum(k - 1, 0)
            p = (before >= NB).astype(jnp.int32)
            j = before - NB * p

            @pl.when(hub)
            def _():
                forward(m)

            @pl.when(jnp.logical_and(jnp.logical_not(hub), m >= 0))
            def _():
                slab_copy(m).wait_recv()

            @pl.when(jnp.logical_and(q == 0, k > 0))
            def _():
                update(p, j, 0, B)

            @pl.when(jnp.logical_and(q == 1, k < 2 * NB - 1))
            def _():
                middle(k, (k >= NB).astype(jnp.int32))

            @pl.when(m == NS - 2)
            def _():
                acc[...] = dot(vt[1, :, pl.ds(0, B - HALF)], xs[block_rows(2 * NB - 1, 0, B - HALF), :])

            return carry

        lax.fori_loop(0, NS + AHEAD, slot, 0)
        rest = dot(vt[1, :, pl.ds(B - HALF, HALF)], xs[block_rows(2 * NB - 1, B - HALF, HALF), :])
        mb[...] = masked(acc[...] + rest, 1)
        update(1, NB - 1, 0, B)

        @pl.when(hub)
        def _():
            drain(slab_out.at[0], 2 * NB)
            stat_copy(4, sibling).wait_send()
            stat_sends(lambda d: stat_copy(d, around[d]).wait_send())
            for number, trees in enumerate(ROLES):
                @pl.when(role == number)
                def _():
                    for t, (_, children) in enumerate(trees):
                        for d in children:
                            drain(tree_out.at[t, d], NB // 2)

            @pl.when(jnp.logical_or(z > 0, y > 0))
            def _():
                best_copy(1, 2, sibling).wait_send()

        @pl.when(jnp.logical_not(hub))
        def _():
            stat_copy(0, sibling).wait_recv()

    @pl.when(jnp.logical_not(hub))
    def _():
        best_copy(0, 1, sibling).wait_send()

    stat[...] = st[...]


def place_kernel(res, stat, perm, out, var, imp, lines, slots, sems):
    scores = pltpu.make_async_copy(stat.at[pl.ds(0, 4)], lines, sems.at[PARTS])
    scores.start()
    owners = pltpu.make_async_copy(perm, slots, sems.at[PARTS + 1])
    owners.start()
    step = B // PARTS
    parts = [pltpu.make_async_copy(res.at[pl.ds(r * step, step)], out.at[pl.ds(r * step, step)], sems.at[r]) for r in range(PARTS)]
    for part in parts:
        part.start()
    var[...] = stat[4, pl.ds(0, 12), :]
    scores.wait()
    owners.wait()
    for i in range(imp.shape[0]):
        site = slots[i]
        line = lax.shift_right_logical(site, 7)
        plane = lax.shift_right_logical(line * 43, 9)
        imp[i] = lines[plane, line - 12 * plane, jnp.bitwise_and(site, 127)]
    for part in parts:
        part.wait()


def shards(cross_cov, diag_inverse, factor_u, factor_v, rank_ids, weights_obs, observations, prior_var, incumbent, owner_perm):
    hbm = pl.BlockSpec(memory_space=pltpu.HBM)
    vmem = pl.BlockSpec(memory_space=pltpu.VMEM)
    dma = pltpu.SemaphoreType.DMA
    solved, stats = pl.pallas_call(
        solve_kernel,
        name="solve",
        out_shape=(pltpu.VMEM((B, B), BF), pltpu.VMEM((5, 16, 128), F32)),
        in_specs=[hbm] * 9,
        out_specs=(vmem, vmem),
        scratch_shapes=[
            pltpu.VMEM((2 * NB * B, W), BF),
            pltpu.VMEM((2, B, R), BF),
            pltpu.VMEM((2, B, R), BF),
            pltpu.VMEM((2, R, B), BF),
            pltpu.VMEM((B, B), BF),
            pltpu.VMEM((R, W), BF),
            pltpu.VMEM((R, W), F32),
            pltpu.VMEM((24, 128), F32),
            pltpu.VMEM((12, 128), F32),
            pltpu.VMEM((12, 128), F32),
            pltpu.VMEM((5, 16, 128), F32),
            pltpu.VMEM((2, 16, 128), F32),
            pltpu.VMEM((2, 16, 128), F32),
            pltpu.VMEM((8, 8, 128), F32),
            pltpu.SMEM((1, 2), jnp.int32),
            pltpu.SMEM((1,), jnp.int32),
            dma((23,)),
            dma((NS * 4,)),
            dma((NS,)),
            dma((4, 4)),
            dma((1,)),
            dma((8,)),
            dma((3,)),
            dma,
            dma((5,)),
            dma((4,)),
            dma((4,)),
        ],
        compiler_params=pltpu.CompilerParams(collective_id=0, has_side_effects=True, vmem_limit_bytes=48 << 20),
        cost_estimate=pl.CostEstimate(flops=7_250_000_000, bytes_accessed=9_400_000, transcendentals=0),
    )(
        *(
            pltpu.with_memory_space_constraint(array, pltpu.HBM)
            for array in (
                cross_cov, diag_inverse, factor_u, factor_v, rank_ids, weights_obs.reshape(24, 128),
                observations.reshape(12, 128), prior_var.reshape(12, 128),
            )
        ),
        incumbent,
    )
    slots = owner_perm.shape[0]
    result, reduction, improvement = pl.pallas_call(
        place_kernel,
        name="place",
        out_shape=(
            jax.ShapeDtypeStruct((B, B), BF),
            jax.ShapeDtypeStruct((12, 128), F32),
            jax.ShapeDtypeStruct((slots,), F32),
        ),
        in_specs=[vmem, vmem, hbm],
        out_specs=(hbm, vmem, pl.BlockSpec(memory_space=pltpu.SMEM)),
        scratch_shapes=[pltpu.SMEM((4, 16, 128), F32), pltpu.SMEM((slots,), jnp.int32), dma((PARTS + 2,))],
        compiler_params=pltpu.CompilerParams(vmem_limit_bytes=16 << 20),
    )(solved, stats, pltpu.with_memory_space_constraint(owner_perm, pltpu.HBM))
    return result, reduction.reshape(B), improvement


def solution(mesh):
    placed = (
        P("row", "col"), P(), P(None, "row", None), P(None, "row", None), P("row", None),
        P(), P("row"), P("col"), P(), P(("row", "col")),
    )
    return jax.shard_map(
        shards, mesh=mesh, in_specs=placed, out_specs=(P("row", "col"), P("col"), P(("row", "col"))), check_vma=False
    )
```
